32 devices in a mesh: ingest: 4 (over x, core), pair: 8 (over z, y).
Axes of the slice: x: 2, y: 2, z: 4, core: 2. Of those that a mesh axis runs over, the one named last changes fastest.
Arguments:
- embeddings: bfloat16 [12288, 768], P(('ingest', 'pair')), may hold values from -8 to 8
- centroids: bfloat16 [16, 768], replicated, may hold values from -6 to 6
- cluster: int32 [12288], P(('ingest', 'pair')), may hold values from 0 to 15, as said below
- labels: int32 [12288], P(('ingest', 'pair')), may hold values from 0 to 127
Outputs:
- weight: float32 [12288], P(('ingest', 'pair'))
- label_sums: float32 [12288, 128], P(('ingest', 'pair'))
The draws below stay inside these ranges and needn't reach their ends.
Inputs may be any that keep to these rules, and one draw needn't show every extreme that they name: Among the rows of one device, at most 192 name clusters of the same ingest index (the same cluster // 4). Among the rows of one device, at most 96 name the same cluster.
All inputs are finite; a program needn't handle non-finite values.
Results may differ from the reference program's by a relative error of at most 0.0014.
Values may be sent and summed in bfloat16 or wider, within the bound.
A program may use at most 64 MiB of HBM per device.

```python
import math
import jax
import jax.numpy as jnp
import numpy as np
from jax import lax

D = 768
LABELS = 128
ROWS_DEV = 384
GROUP_CLUSTERS = 4
CAP = 192
ROWS = 12288
CLUSTERS = 16
CLUSTER_CAP = 96
N_INGEST = 4
DEVICES = 32


def draw_embeddings(key, part):
    prototype_count = 16
    first = jax.random.randint(jax.random.fold_in(key, 21), (ROWS,), 0, prototype_count)
    second = jax.random.randint(jax.random.fold_in(key, 22), (ROWS,), 0, prototype_count)
    chosen = jnp.minimum(first, second)
    copied = jax.random.randint(jax.random.fold_in(key, 23), (ROWS,), 0, 20) < 7
    prototypes = jax.random.normal(jax.random.fold_in(key, 24), (prototype_count, D), jnp.float32)
    spread = 0.1 * jnp.exp(jax.random.uniform(jax.random.fold_in(key, 25), (ROWS, 1), jnp.float32) * math.log(4.7))
    noise = jax.random.normal(jax.random.fold_in(key, 26), (ROWS, D), jnp.float32)
    fresh = jax.random.normal(jax.random.fold_in(key, 28), (ROWS, D), jnp.float32)
    near = prototypes[chosen] + spread * noise
    return jnp.clip(jnp.where(copied[:, None], near, fresh), -8.0, 8.0).astype(jnp.bfloat16)


def draw_cluster(key, part):
    largest = jax.random.randint(jax.random.fold_in(key, 11), (), 0, CLUSTERS)
    largest_group = largest // GROUP_CLUSTERS
    group_weight = jnp.left_shift(jnp.int32(1), jax.random.randint(jax.random.fold_in(key, 12), (N_INGEST,), 0, 4))
    cluster_weight = jnp.left_shift(jnp.int32(1), jax.random.randint(jax.random.fold_in(key, 13), (CLUSTERS,), 0, 4))
    group_pool = N_INGEST * CAP
    cluster_pool = GROUP_CLUSTERS * CLUSTER_CAP

    def one_device(index):
        device_key = jax.random.fold_in(jax.random.fold_in(key, 14), index)
        group_slot = jnp.arange(group_pool, dtype=jnp.int32)
        slot_group = group_slot // CAP
        raw = jax.random.randint(jax.random.fold_in(device_key, 1), (group_pool,), 0, 4096)
        score = raw * group_weight[slot_group] * group_pool + group_slot
        score = jnp.where(slot_group == largest_group, score + (1 << 29), score)
        end_slot = (group_slot == (N_INGEST - 1) * CAP) | (group_slot == 0)
        score = jnp.where(end_slot, score + (1 << 28), score)
        unused, picked = lax.top_k(score, ROWS_DEV)
        order = jax.random.permutation(jax.random.fold_in(device_key, 2), ROWS_DEV)
        row_group = slot_group[picked][order]
        pool_slot = jnp.arange(cluster_pool, dtype=jnp.int32)
        pool_cluster = jnp.arange(N_INGEST, dtype=jnp.int32)[:, None] * GROUP_CLUSTERS + (pool_slot // CLUSTER_CAP)[None, :]
        raw_pool = jax.random.randint(jax.random.fold_in(device_key, 3), (N_INGEST, cluster_pool), 0, 4096)
        pool_score = raw_pool * cluster_weight[pool_cluster] * cluster_pool + pool_slot[None, :]
        pool_score = jnp.where(pool_cluster == largest, pool_score + (1 << 29), pool_score)
        end_cluster = (pool_cluster == CLUSTERS - 1) | (pool_cluster == 0)
        pool_score = jnp.where(end_cluster, pool_score + (1 << 28), pool_score)
        unused_sorted, ranked = lax.top_k(pool_score, cluster_pool)
        ranked_cluster = jnp.take_along_axis(pool_cluster, ranked, axis=1)
        hits = (row_group[:, None] == jnp.arange(N_INGEST, dtype=jnp.int32)[None, :]).astype(jnp.int32)
        rank = jnp.sum((jnp.cumsum(hits, axis=0) - 1) * hits, axis=1)
        return ranked_cluster[row_group, rank]
    return jax.vmap(one_device)(jnp.arange(DEVICES, dtype=jnp.int32)).reshape(ROWS).astype(jnp.int32)


def set_ends(array, own_key, smallest, top_value):
    spot = [jax.random.randint(jax.random.fold_in(own_key, axis), (), 0, length) for axis, length in enumerate(array.shape)]
    main_axis = array.shape.index(max(array.shape))
    beside = spot[:main_axis] + [(spot[main_axis] + 1) % array.shape[main_axis]] + spot[main_axis + 1:]
    return array.at[tuple(spot)].set(smallest).at[tuple(beside)].set(top_value)


def cumulative_ranks(amount, lean):
    weights = [(1 << 20) // math.isqrt(grade ** lean) + 1 for grade in range(1, amount + 1)]
    width = 1 + sum(weights) // (1 << 30)
    return np.cumsum(np.array([max(1, weight // width) for weight in weights]))


def ranked_ids(rng, dims, count, skew):
    listing = cumulative_ranks(count, skew)
    lot = jax.random.randint(jax.random.fold_in(rng, 1), dims, 0, int(listing[count - 1]))
    rank = jnp.searchsorted(jnp.asarray(listing, jnp.int32), lot, side="right")
    return jax.random.permutation(jax.random.fold_in(rng, 2), count)[rank].astype(jnp.int32)


def scatter_about(key, extent, scale, bound, kind=jnp.bfloat16):
    return jnp.clip(scale * jax.random.normal(key, extent, jnp.float32), -bound, bound).astype(kind)


def setup_inputs(seed: int = 0) -> dict:
    streams_of = jax.random.split(jax.random.key(seed), 5)
    return {
        "embeddings": draw_embeddings(jax.random.fold_in(streams_of[4], 71), 0),
        "centroids": scatter_about(streams_of[1], (CLUSTERS, D), 1.0, 6.0),
        "cluster": draw_cluster(jax.random.fold_in(streams_of[4], 71), 0),
        "labels": set_ends(ranked_ids(streams_of[3], (ROWS,), LABELS, 2), jax.random.fold_in(streams_of[3], 3), 0, LABELS - 1).astype(jnp.int32),
    }


SHARPNESS = 8.0
EPSILON = 1e-06

def reference(embeddings, centroids, cluster, labels):
    shifted = centroids[cluster].astype(jnp.float32) + embeddings.astype(jnp.float32)
    unit = (shifted * lax.rsqrt(lax.optimization_barrier(jnp.sum(shifted * shifted, axis=1, keepdims=True)) + EPSILON)).astype(jnp.bfloat16)
    key_rows = unit.astype(jnp.float32)
    table = (labels[:, None] == jnp.arange(LABELS, dtype=jnp.int32)[None, :]).astype(jnp.float32)
    block_rows = math.gcd(ROWS, 512)

    def one_block(first_row):
        queries = lax.dynamic_slice_in_dim(key_rows, first_row, block_rows, 0)
        query_cluster = lax.dynamic_slice_in_dim(cluster, first_row, block_rows, 0)
        scores = jnp.dot(queries, key_rows.T, precision=lax.Precision.HIGHEST)
        kernel = jnp.where(query_cluster[:, None] == cluster[None, :], jnp.exp(SHARPNESS * (scores - 1.0)), 0.0)
        density = lax.optimization_barrier(jnp.sum(kernel, axis=1))
        rounded = kernel.astype(jnp.bfloat16).astype(jnp.float32)
        label_part = jnp.dot(rounded, table, precision=lax.Precision.HIGHEST)
        return (density, label_part)
    starts = (jnp.arange(ROWS // block_rows) * block_rows).astype(jnp.int32)
    density, label_sums = lax.map(one_block, starts)
    density = density.reshape(ROWS)
    label_sums = label_sums.reshape(ROWS, LABELS)
    return (1.0 / density, label_sums)
```

```python
import functools

import jax
import jax.numpy as jnp
from jax import lax
from jax.experimental import pallas as pl
from jax.experimental.pallas import tpu as pltpu
from jax.sharding import PartitionSpec as P

LABELS = 128
SHARPNESS = 8.0
EPSILON = 1e-06
CORES = 2
MESH = pl.DeviceIdType.MESH


class Plan:
    def __init__(self, mesh_shape, rows, width, clusters):
        self.groups = mesh_shape["ingest"]
        self.sub = mesh_shape["pair"] // self.groups
        self.xs = mesh_shape["ingest"] // CORES
        self.rows = rows
        self.width = width
        self.clusters = clusters
        self.group_clusters = clusters // self.groups
        self.cap = 2 * rows // self.groups
        self.slots = self.groups * self.cap
        self.places = self.xs * self.sub * CORES
        self.chunk = 256 if self.slots % 256 == 0 else 128

    def place(self, dx, dy, dc):
        return (dx % self.xs * self.sub + dy % self.sub) * CORES + dc % CORES

    def offsets(self):
        return [
            (dx, dy, dc)
            for dx in range(self.xs)
            for dy in range(self.sub)
            for dc in range(CORES)
            if dx or dy or dc
        ]


def group_of(plan, cluster):
    group = jnp.zeros(cluster.shape, jnp.int32)
    for g in range(1, plan.groups):
        group = group + (cluster >= g * plan.group_clusters).astype(jnp.int32)
    return group


def column_of(row):
    parts = []
    eye = lax.broadcasted_iota(jnp.int32, (128, 128), 0) == lax.broadcasted_iota(
        jnp.int32, (128, 128), 1
    )
    for b in range(row.shape[1] // 128):
        parts.append(
            jnp.sum(jnp.where(eye, row[:, b * 128 : (b + 1) * 128], 0), axis=1, keepdims=True)
        )
    return jnp.concatenate(parts, axis=0)


def row_of(column):
    parts = []
    eye = lax.broadcasted_iota(jnp.int32, (128, 128), 0) == lax.broadcasted_iota(
        jnp.int32, (128, 128), 1
    )
    for b in range(column.shape[0] // 128):
        parts.append(
            jnp.sum(jnp.where(eye, column[b * 128 : (b + 1) * 128, :], 0), axis=0, keepdims=True)
        )
    return jnp.concatenate(parts, axis=1)


def kernel(
    plan,
    emb_ref,
    cent_ref,
    ccol_ref,
    crow_ref,
    lcol_ref,
    weight_ref,
    label_ref,
    packed,
    keys,
    codes,
    code_tx,
    code_rx,
    qcol,
    poscol,
    dens_acc,
    lab_acc,
    dens_tx,
    dens_rx,
    lab_rx,
    send_sem,
    row_sem,
    code_rx_sem,
    code_sem,
    dens_sem,
    lab_sem,
):
    G, cap, slots, sub = plan.groups, plan.cap, plan.slots, plan.sub
    ingest = lax.axis_index("ingest")
    pair = lax.axis_index("pair")
    x, core = ingest // CORES, ingest % CORES
    z, y = pair // sub, pair % sub

    def plane_device(dx, dy, dc):
        return (
            lax.rem(x + dx, plan.xs) * CORES + lax.rem(core + dc, CORES),
            z * sub + lax.rem(y + dy, sub),
        )

    def column_device(dz):
        return (ingest, lax.rem(z + dz, G) * sub + y)

    barrier = pltpu.get_barrier_semaphore()
    for dz in range(1, G):
        pl.semaphore_signal(barrier, inc=1, device_id=column_device(dz), device_id_type=MESH)
    for offset in plan.offsets():
        pl.semaphore_signal(barrier, inc=1, device_id=plane_device(*offset), device_id_type=MESH)

    def slot_of(cluster, rank):
        block = z - group_of(plan, cluster)
        block = jnp.where(block < 0, block + G, block)
        return block * cap + rank

    rows = plan.rows
    ccol, crow = ccol_ref[...], crow_ref[...]
    same = group_of(plan, ccol) == group_of(plan, crow)
    first = lax.broadcasted_iota(jnp.int32, (rows, rows), 0)
    second = lax.broadcasted_iota(jnp.int32, (rows, rows), 1)
    rank_row = jnp.sum(jnp.where(same & (first < second), 1, 0), axis=0, keepdims=True)
    rank_col = jnp.sum(jnp.where(same & (second < first), 1, 0), axis=1, keepdims=True)
    pos_row = slot_of(crow, rank_row)
    pos_col = slot_of(ccol, rank_col)
    poscol[...] = pos_col
    code_col = ccol * LABELS + lcol_ref[...] + 1
    lane = lax.broadcasted_iota(jnp.int32, (rows, slots), 1)
    code_tx[...] = jnp.sum(jnp.where(pos_col == lane, code_col, 0), axis=0, keepdims=True)

    lookup = (ccol == lax.broadcasted_iota(jnp.int32, (rows, plan.clusters), 1)).astype(
        jnp.float32
    ).astype(jnp.bfloat16)
    centre = jnp.dot(lookup, cent_ref[...], preferred_element_type=jnp.float32)
    shifted = centre + emb_ref[...].astype(jnp.float32)
    scale = lax.rsqrt(jnp.sum(shifted * shifted, axis=1, keepdims=True) + EPSILON)
    unit = (shifted * scale).astype(jnp.bfloat16)
    for b in range(G):
        pick = (
            lax.broadcasted_iota(jnp.int32, (cap, rows), 0) + b * cap == pos_row
        ).astype(jnp.float32).astype(jnp.bfloat16)
        block = jnp.dot(pick, unit, preferred_element_type=jnp.float32).astype(jnp.bfloat16)
        if b == 0:
            keys[0, pl.ds(0, cap), :] = block
        else:
            packed[pl.ds(b * cap, cap), :] = block

    pl.semaphore_wait(barrier, G - 1 + plan.places - 1)

    sent = []

    def send(src, dst, sem, device):
        copy = pltpu.make_async_remote_copy(
            src_ref=src,
            dst_ref=dst,
            send_sem=send_sem.at[len(sent)],
            recv_sem=sem,
            device_id=device,
            device_id_type=MESH,
        )
        copy.start()
        sent.append(copy)

    def arrive(dst, sem):
        pltpu.make_async_remote_copy(
            src_ref=dst,
            dst_ref=dst,
            send_sem=send_sem.at[0],
            recv_sem=sem,
            device_id=column_device(1),
            device_id_type=MESH,
        ).wait_recv()

    def part(place, b):
        return keys.at[place, pl.ds(b * cap, cap)]

    def pass_on(src_place, to_place, b, device):
        send(part(src_place, b), part(to_place, b), row_sem.at[to_place, b], device)

    def rows_arrive(place, b):
        arrive(part(place, b), row_sem.at[place, b])

    xrange, yrange = range(1, plan.xs), range(1, sub)

    def spread(b):
        for dx in xrange:
            pass_on(0, plan.place(-dx, 0, 0), b, plane_device(dx, 0, 0))
        for dy in yrange:
            pass_on(0, plan.place(0, -dy, 0), b, plane_device(0, dy, 0))
        pass_on(0, plan.place(0, 0, 1), b, plane_device(0, 0, 1))

    def forward_near(b):
        for dx in xrange:
            rows_arrive(plan.place(dx, 0, 0), b)
            if b % 2 == 0:
                for dy in yrange:
                    pass_on(
                        plan.place(dx, 0, 0), plan.place(dx, -dy, 0), b, plane_device(0, dy, 0)
                    )
            pass_on(plan.place(dx, 0, 0), plan.place(dx, 0, 1), b, plane_device(0, 0, 1))
        for dy in yrange:
            rows_arrive(plan.place(0, dy, 0), b)
            if b % 2 == 1:
                for dx in xrange:
                    pass_on(
                        plan.place(0, dy, 0), plan.place(-dx, dy, 0), b, plane_device(dx, 0, 0)
                    )
            pass_on(plan.place(0, dy, 0), plan.place(0, dy, 1), b, plane_device(0, 0, 1))

    def forward_far(b):
        for dx in xrange:
            for dy in yrange:
                rows_arrive(plan.place(dx, dy, 0), b)
                pass_on(plan.place(dx, dy, 0), plan.place(dx, dy, 1), b, plane_device(0, 0, 1))

    for b in range(1, G):
        send(code_tx, code_rx.at[b], code_rx_sem.at[b], column_device(G - b))
    for b in range(1, G):
        send(
            packed.at[pl.ds(b * cap, cap)], part(0, b), row_sem.at[0, b], column_device(G - b)
        )
    spread(0)

    lane_row = lax.broadcasted_iota(jnp.int32, (1, slots), 1)

    def block_lanes(b):
        return (lane_row >= b * cap) & (lane_row < (b + 1) * cap)

    code = jnp.where(block_lanes(0), code_tx[...], 0)
    for b in range(1, G):
        arrive(code_rx.at[b], code_rx_sem.at[b])
        code = code + jnp.where(block_lanes(b), code_rx[b], 0)
    codes[0] = code
    for offset in plan.offsets():
        to = plan.place(*(-step for step in offset))
        send(codes.at[0], codes.at[to], code_sem.at[to], plane_device(*offset))
    qcol[...] = (column_of(code) - 1) >> 7
    dens_acc[...] = jnp.zeros_like(dens_acc)
    lab_acc[...] = jnp.zeros_like(lab_acc)
    for offset in plan.offsets():
        arrive(codes.at[plan.place(*offset)], code_sem.at[plan.place(*offset)])

    chunk = plan.chunk
    steps = slots // chunk

    def compute(place):
        def body(step, carry):
            start = pl.multiple_of(step * chunk, chunk)
            key_rows = keys[place, pl.ds(start, chunk), :]
            key_code = codes[place, :, pl.ds(start, chunk)] - 1
            scores = lax.dot_general(
                keys[0], key_rows, (((1,), (1,)), ((), ())), preferred_element_type=jnp.float32
            )
            value = jnp.where(
                qcol[...] == key_code >> 7,
                jnp.exp(SHARPNESS * scores - SHARPNESS),
                0.0,
            )
            part_sum = value[:, :128]
            for b in range(1, chunk // 128):
                part_sum = part_sum + value[:, b * 128 : (b + 1) * 128]
            dens_acc[...] += part_sum
            table = (
                lax.broadcasted_iota(jnp.int32, (LABELS, chunk), 0) == (key_code & (LABELS - 1))
            ).astype(jnp.float32).astype(jnp.bfloat16)
            lab_acc[...] += lax.dot_general(
                value.astype(jnp.bfloat16),
                table,
                (((1,), (1,)), ((), ())),
                preferred_element_type=jnp.float32,
            )
            return carry

        lax.fori_loop(0, steps, body, 0)

    for b in range(1, G):
        rows_arrive(0, b)
        spread(b)
        forward_near(b - 1)
        if b >= 2:
            forward_far(b - 2)

    def arrived(place):
        for b in range(G):
            rows_arrive(place, b)

    forward_far(G - 2)
    compute(0)
    forward_near(G - 1)
    arrived(plan.place(0, 0, 1))
    compute(plan.place(0, 0, 1))
    near = [(dx, 0) for dx in xrange] + [(0, dy) for dy in yrange]
    for dx, dy in near:
        compute(plan.place(dx, dy, 0))
    forward_far(G - 1)
    for dx, dy in near:
        arrived(plan.place(dx, dy, 1))
        compute(plan.place(dx, dy, 1))
    for dx in xrange:
        for dy in yrange:
            compute(plan.place(dx, dy, 0))
            arrived(plan.place(dx, dy, 1))
            compute(plan.place(dx, dy, 1))

    for b in range(1, G):
        send(
            lab_acc.at[pl.ds(b * cap, cap)],
            lab_rx.at[pl.ds(b * cap, cap)],
            lab_sem.at[b],
            column_device(b),
        )
    dens_row = row_of(jnp.sum(dens_acc[...], axis=1, keepdims=True))
    dens_tx[...] = dens_row
    for b in range(1, G):
        send(dens_tx, dens_rx.at[b], dens_sem.at[b], column_device(b))
    lab_rx[pl.ds(0, cap), :] = lab_acc[pl.ds(0, cap), :]
    dens = jnp.where(block_lanes(0), dens_row, 0.0)
    for b in range(1, G):
        arrive(dens_rx.at[b], dens_sem.at[b])
        dens = dens + jnp.where(block_lanes(b), dens_rx[b], 0.0)
    hit = poscol[...] == lane
    weight_ref[...] = row_of(1.0 / jnp.sum(jnp.where(hit, dens, 0.0), axis=1, keepdims=True))
    for b in range(1, G):
        arrive(lab_rx.at[pl.ds(b * cap, cap)], lab_sem.at[b])
    pick = hit.astype(jnp.float32).astype(jnp.bfloat16)
    rest = lab_rx[...]
    total = jnp.zeros((rows, LABELS), jnp.float32)
    for _ in range(3):
        piece = rest.astype(jnp.bfloat16)
        total = total + jnp.dot(pick, piece, preferred_element_type=jnp.float32)
        rest = rest - piece.astype(jnp.float32)
    label_ref[...] = total
    for copy in sent:
        copy.wait_send()


def on_device(mesh_shape, embeddings, centroids, cluster, labels):
    rows, width = embeddings.shape
    plan = Plan(mesh_shape, rows, width, centroids.shape[0])
    G, places = plan.groups, plan.places
    near, far = plan.xs - 1 + plan.sub - 1, (plan.xs - 1) * (plan.sub - 1)
    copies = 4 * (G - 1) + places - 1 + G * (near + 1 + near + far + far)
    vmem = pl.BlockSpec(memory_space=pltpu.VMEM)
    weight, label_sums = pl.pallas_call(
        functools.partial(kernel, plan),
        out_shape=(
            jax.ShapeDtypeStruct((1, rows), jnp.float32),
            jax.ShapeDtypeStruct((rows, LABELS), jnp.float32),
        ),
        in_specs=[vmem] * 5,
        out_specs=(vmem, vmem),
        scratch_shapes=[
            pltpu.VMEM((plan.slots, width), jnp.bfloat16),
            pltpu.VMEM((places, plan.slots, width), jnp.bfloat16),
            pltpu.VMEM((places, 1, plan.slots), jnp.int32),
            pltpu.VMEM((1, plan.slots), jnp.int32),
            pltpu.VMEM((G, 1, plan.slots), jnp.int32),
            pltpu.VMEM((plan.slots, 1), jnp.int32),
            pltpu.VMEM((rows, 1), jnp.int32),
            pltpu.VMEM((plan.slots, 128), jnp.float32),
            pltpu.VMEM((plan.slots, LABELS), jnp.float32),
            pltpu.VMEM((1, plan.slots), jnp.float32),
            pltpu.VMEM((G, 1, plan.slots), jnp.float32),
            pltpu.VMEM((plan.slots, LABELS), jnp.float32),
            pltpu.SemaphoreType.DMA((copies,)),
            pltpu.SemaphoreType.DMA((places, G)),
            pltpu.SemaphoreType.DMA((G,)),
            pltpu.SemaphoreType.DMA((places,)),
            pltpu.SemaphoreType.DMA((G,)),
            pltpu.SemaphoreType.DMA((G,)),
        ],
        compiler_params=pltpu.CompilerParams(
            collective_id=0, has_side_effects=True, vmem_limit_bytes=48 * 1024 * 1024
        ),
    )(
        embeddings,
        centroids,
        cluster.reshape(rows, 1),
        cluster.reshape(1, rows),
        labels.reshape(rows, 1),
    )
    return (weight.reshape(rows), label_sums)


def solution(mesh):
    in_specs = (P(("ingest", "pair"), None), P(), P(("ingest", "pair")), P(("ingest", "pair")))
    out_specs = (P(("ingest", "pair")), P(("ingest", "pair"), None))
    return jax.shard_map(
        functools.partial(on_device, dict(mesh.shape)),
        mesh=mesh,
        in_specs=in_specs,
        out_specs=out_specs,
        check_vma=False,
    )
```

```python
import functools

import jax
import jax.numpy as jnp
from jax import lax
from jax.experimental import pallas as pl
from jax.experimental.pallas import tpu as pltpu
from jax.sharding import PartitionSpec as P

LABELS = 128
SHARPNESS = 8.0
EPSILON = 1e-06
CORES = 2
MESH = pl.DeviceIdType.MESH


class Plan:
    def __init__(self, mesh_shape, rows, width, clusters):
        self.groups = mesh_shape["ingest"]
        self.sub = mesh_shape["pair"] // self.groups
        self.xs = mesh_shape["ingest"] // CORES
        self.rows = rows
        self.width = width
        self.clusters = clusters
        self.group_clusters = clusters // self.groups
        self.cap = 2 * rows // self.groups
        self.slots = self.groups * self.cap
        self.places = self.xs * self.sub * CORES
        self.order = sorted(range(self.groups), key=lambda o: (min(o, self.groups - o), o))
        self.chunk = 256 if self.slots % 256 == 0 else 128

    def place(self, dx, dy, dc):
        return (dx % self.xs * self.sub + dy % self.sub) * CORES + dc % CORES

    def offsets(self):
        return [
            (dx, dy, dc)
            for dx in range(self.xs)
            for dy in range(self.sub)
            for dc in range(CORES)
            if dx or dy or dc
        ]


def group_of(plan, cluster):
    group = jnp.zeros(cluster.shape, jnp.int32)
    for g in range(1, plan.groups):
        group = group + (cluster >= g * plan.group_clusters).astype(jnp.int32)
    return group


def column_of(row):
    parts = []
    eye = lax.broadcasted_iota(jnp.int32, (128, 128), 0) == lax.broadcasted_iota(
        jnp.int32, (128, 128), 1
    )
    for b in range(row.shape[1] // 128):
        parts.append(
            jnp.sum(jnp.where(eye, row[:, b * 128 : (b + 1) * 128], 0), axis=1, keepdims=True)
        )
    return jnp.concatenate(parts, axis=0)


def row_of(column):
    parts = []
    eye = lax.broadcasted_iota(jnp.int32, (128, 128), 0) == lax.broadcasted_iota(
        jnp.int32, (128, 128), 1
    )
    for b in range(column.shape[0] // 128):
        parts.append(
            jnp.sum(jnp.where(eye, column[b * 128 : (b + 1) * 128, :], 0), axis=0, keepdims=True)
        )
    return jnp.concatenate(parts, axis=1)


def kernel(
    plan,
    emb_ref,
    cent_ref,
    code_ref,
    weight_ref,
    label_ref,
    emb,
    packed,
    keys,
    codes,
    code_tx,
    code_rx,
    qcol,
    poscol,
    dens_acc,
    lab_acc,
    dens_tx,
    dens_rx,
    lab_rx,
    send_sem,
    row_sem,
    code_rx_sem,
    code_sem,
    dens_sem,
    lab_sem,
    emb_sem,
):
    G, cap, slots, sub, order = plan.groups, plan.cap, plan.slots, plan.sub, plan.order
    ingest = lax.axis_index("ingest")
    pair = lax.axis_index("pair")
    x, core = ingest // CORES, ingest % CORES
    z, y = pair // sub, pair % sub

    def plane_device(dx, dy, dc):
        return (
            lax.rem(x + dx, plan.xs) * CORES + lax.rem(core + dc, CORES),
            z * sub + lax.rem(y + dy, sub),
        )

    def column_device(dz):
        return (ingest, lax.rem(z + dz, G) * sub + y)

    fetch = pltpu.make_async_copy(emb_ref, emb, emb_sem)
    fetch.start()
    barrier = pltpu.get_barrier_semaphore()
    for dz in range(1, G):
        pl.semaphore_signal(barrier, inc=1, device_id=column_device(dz), device_id_type=MESH)
    for offset in plan.offsets():
        pl.semaphore_signal(barrier, inc=1, device_id=plane_device(*offset), device_id_type=MESH)

    def slot_of(cluster, rank):
        offset = z - group_of(plan, cluster)
        offset = jnp.where(offset < 0, offset + G, offset)
        block = jnp.zeros(offset.shape, jnp.int32)
        for b in range(1, G):
            block = jnp.where(offset == order[b], b, block)
        return block * cap + rank

    rows = plan.rows
    code_row = code_ref[...]
    code_col = column_of(code_row)
    crow, ccol = code_row >> 7, code_col >> 7
    same = group_of(plan, ccol) == group_of(plan, crow)
    first = lax.broadcasted_iota(jnp.int32, (rows, rows), 0)
    second = lax.broadcasted_iota(jnp.int32, (rows, rows), 1)
    rank_row = jnp.sum(jnp.where(same & (first < second), 1, 0), axis=0, keepdims=True)
    rank_col = jnp.sum(jnp.where(same & (second < first), 1, 0), axis=1, keepdims=True)
    pos_row = slot_of(crow, rank_row)
    pos_col = slot_of(ccol, rank_col)
    poscol[...] = pos_col
    lane = lax.broadcasted_iota(jnp.int32, (rows, slots), 1)
    code_tx[...] = jnp.sum(jnp.where(pos_col == lane, code_col + 1, 0), axis=0, keepdims=True)

    lookup = (ccol == lax.broadcasted_iota(jnp.int32, (rows, plan.clusters), 1)).astype(
        jnp.float32
    ).astype(jnp.bfloat16)
    centre = jnp.dot(lookup, cent_ref[...], preferred_element_type=jnp.float32)
    fetch.wait()
    shifted = centre + emb[...].astype(jnp.float32)
    scale = lax.rsqrt(jnp.sum(shifted * shifted, axis=1, keepdims=True) + EPSILON)
    unit = (shifted * scale).astype(jnp.bfloat16)
    for b in range(G):
        pick = (
            lax.broadcasted_iota(jnp.int32, (cap, rows), 0) + b * cap == pos_row
        ).astype(jnp.float32).astype(jnp.bfloat16)
        block = jnp.dot(pick, unit, preferred_element_type=jnp.float32).astype(jnp.bfloat16)
        if b == 0:
            keys[0, pl.ds(0, cap), :] = block
        else:
            packed[pl.ds(b * cap, cap), :] = block

    pl.semaphore_wait(barrier, G - 1 + plan.places - 1)

    sent, dispatched = [], []

    def send(src, dst, sem, device):
        copy = pltpu.make_async_remote_copy(
            src_ref=src,
            dst_ref=dst,
            send_sem=send_sem.at[len(sent)],
            recv_sem=sem,
            device_id=device,
            device_id_type=MESH,
        )
        copy.start()
        sent.append(copy)

    def arrive(dst, sem):
        pltpu.make_async_remote_copy(
            src_ref=dst,
            dst_ref=dst,
            send_sem=send_sem.at[0],
            recv_sem=sem,
            device_id=column_device(1),
            device_id_type=MESH,
        ).wait_recv()

    def part(place, b, half=None):
        if half is None:
            return keys.at[place, pl.ds(b * cap, cap)]
        return keys.at[place, pl.ds(b * cap + half * (cap // 2), cap // 2)]

    def pass_on(src_place, to_place, b, device, half=None):
        send(part(src_place, b, half), part(to_place, b, half), row_sem.at[to_place, b], device)

    here = {(0, 0)}

    def rows_arrive(place, b):
        if (place, b) not in here:
            here.add((place, b))
            arrive(part(place, b), row_sem.at[place, b])

    xrange, yrange = range(1, plan.xs), range(1, sub)

    def spread(b):
        for dx in xrange:
            pass_on(0, plan.place(-dx, 0, 0), b, plane_device(dx, 0, 0))
        for dy in yrange:
            pass_on(0, plan.place(0, -dy, 0), b, plane_device(0, dy, 0))
        pass_on(0, plan.place(0, 0, 1), b, plane_device(0, 0, 1))

    def forward_near(b):
        for dx in xrange:
            rows_arrive(plan.place(dx, 0, 0), b)
            for dy in yrange:
                pass_on(
                    plan.place(dx, 0, 0), plan.place(dx, -dy, 0), b, plane_device(0, dy, 0), 0
                )
            pass_on(plan.place(dx, 0, 0), plan.place(dx, 0, 1), b, plane_device(0, 0, 1))
        for dy in yrange:
            rows_arrive(plan.place(0, dy, 0), b)
            for dx in xrange:
                pass_on(
                    plan.place(0, dy, 0), plan.place(-dx, dy, 0), b, plane_device(dx, 0, 0), 1
                )
            pass_on(plan.place(0, dy, 0), plan.place(0, dy, 1), b, plane_device(0, 0, 1))

    def forward_far(b):
        for dx in xrange:
            for dy in yrange:
                rows_arrive(plan.place(dx, dy, 0), b)
                pass_on(plan.place(dx, dy, 0), plan.place(dx, dy, 1), b, plane_device(0, 0, 1))

    def dispatch(b):
        send(
            packed.at[pl.ds(b * cap, cap)],
            part(0, b),
            row_sem.at[0, b],
            column_device(G - order[b]),
        )
        dispatched.append(sent[-1])
        return sent[-1]

    for b in range(1, G):
        send(code_tx, code_rx.at[b], code_rx_sem.at[b], column_device(G - order[b]))
    going = dispatch(1)
    spread(0)

    lane_row = lax.broadcasted_iota(jnp.int32, (1, slots), 1)

    def block_lanes(b):
        return (lane_row >= b * cap) & (lane_row < (b + 1) * cap)

    code = jnp.where(block_lanes(0), code_tx[...], 0)
    for b in range(1, G):
        arrive(code_rx.at[b], code_rx_sem.at[b])
        code = code + jnp.where(block_lanes(b), code_rx[b], 0)
    codes[0] = code
    for offset in plan.offsets():
        to = plan.place(*(-step for step in offset))
        send(codes.at[0], codes.at[to], code_sem.at[to], plane_device(*offset))
    qcol[...] = (column_of(code) - 1) >> 7
    dens_acc[...] = jnp.zeros_like(dens_acc)
    lab_acc[...] = jnp.zeros_like(lab_acc)
    for offset in plan.offsets():
        arrive(codes.at[plan.place(*offset)], code_sem.at[plan.place(*offset)])

    chunk = plan.chunk
    steps = slots // chunk

    def compute(place, first_step, last_step):
        for b in range((last_step * chunk - 1) // cap + 1):
            rows_arrive(place, b)

        def body(step, carry):
            start = pl.multiple_of(step * chunk, chunk)
            key_rows = keys[place, pl.ds(start, chunk), :]
            key_code = codes[place, :, pl.ds(start, chunk)] - 1
            scores = lax.dot_general(
                keys[0], key_rows, (((1,), (1,)), ((), ())), preferred_element_type=jnp.float32
            )
            value = jnp.where(
                qcol[...] == key_code >> 7,
                jnp.exp(SHARPNESS * scores - SHARPNESS),
                0.0,
            )
            part_sum = value[:, :128]
            for b in range(1, chunk // 128):
                part_sum = part_sum + value[:, b * 128 : (b + 1) * 128]
            dens_acc[...] += part_sum
            table = (
                lax.broadcasted_iota(jnp.int32, (LABELS, chunk), 0) == (key_code & (LABELS - 1))
            ).astype(jnp.float32).astype(jnp.bfloat16)
            lab_acc[...] += lax.dot_general(
                value.astype(jnp.bfloat16),
                table,
                (((1,), (1,)), ((), ())),
                preferred_element_type=jnp.float32,
            )
            return carry

        lax.fori_loop(first_step, last_step, body, 0)

    for b in range(1, G):
        going.wait_send()
        if b + 1 < G:
            going = dispatch(b + 1)
        rows_arrive(0, b)
        spread(b)
        forward_near(b - 1)
        if b >= 2:
            forward_far(b - 2)

    near = [(dx, 0) for dx in xrange] + [(0, dy) for dy in yrange]
    far = [(dx, dy) for dx in xrange for dy in yrange]
    compute(0, 0, steps)
    compute(plan.place(0, 0, 1), 0, steps)
    for dx, dy in near:
        compute(plan.place(dx, dy, 0), 0, steps - 1)
    forward_near(G - 1)
    forward_far(G - 2)
    for dx, dy in near:
        compute(plan.place(dx, dy, 1), 0, steps - 1)
    for dc in range(CORES):
        for dx, dy in far:
            compute(plan.place(dx, dy, dc), 0, steps - 1)
    forward_far(G - 1)
    for dx, dy in near + far:
        for dc in range(CORES):
            compute(plan.place(dx, dy, dc), steps - 1, steps)

    dens_row = row_of(jnp.sum(dens_acc[...], axis=1, keepdims=True))
    dens_tx[...] = dens_row
    for b in range(1, G):
        send(dens_tx, dens_rx.at[b], dens_sem.at[b], column_device(order[b]))
    for b in range(1, G):
        send(
            lab_acc.at[pl.ds(b * cap, cap)],
            lab_rx.at[pl.ds(b * cap, cap)],
            lab_sem.at[b],
            column_device(order[b]),
        )
    lab_rx[pl.ds(0, cap), :] = lab_acc[pl.ds(0, cap), :]
    dens = jnp.where(block_lanes(0), dens_row, 0.0)
    for b in range(1, G):
        arrive(dens_rx.at[b], dens_sem.at[b])
        dens = dens + jnp.where(block_lanes(b), dens_rx[b], 0.0)
    hit = poscol[...] == lane
    weight_ref[...] = row_of(1.0 / jnp.sum(jnp.where(hit, dens, 0.0), axis=1, keepdims=True))
    for b in range(1, G):
        arrive(lab_rx.at[pl.ds(b * cap, cap)], lab_sem.at[b])
    pick = hit.astype(jnp.float32).astype(jnp.bfloat16)
    rest = lab_rx[...]
    total = jnp.zeros((rows, LABELS), jnp.float32)
    for _ in range(3):
        piece = rest.astype(jnp.bfloat16)
        total = total + jnp.dot(pick, piece, preferred_element_type=jnp.float32)
        rest = rest - piece.astype(jnp.float32)
    label_ref[...] = total
    for copy in sent:
        if not any(copy is other for other in dispatched):
            copy.wait_send()


def on_device(mesh_shape, embeddings, centroids, cluster, labels):
    rows, width = embeddings.shape
    plan = Plan(mesh_shape, rows, width, centroids.shape[0])
    G, places = plan.groups, plan.places
    near, far = plan.xs - 1 + plan.sub - 1, (plan.xs - 1) * (plan.sub - 1)
    copies = 4 * (G - 1) + places - 1 + G * (near + 1 + near + 2 * far + far)
    vmem = pl.BlockSpec(memory_space=pltpu.VMEM)
    weight, label_sums = pl.pallas_call(
        functools.partial(kernel, plan),
        out_shape=(
            jax.ShapeDtypeStruct((1, rows), jnp.float32),
            jax.ShapeDtypeStruct((rows, LABELS), jnp.float32),
        ),
        in_specs=[pl.BlockSpec(memory_space=pl.ANY), vmem, vmem],
        out_specs=(vmem, vmem),
        scratch_shapes=[
            pltpu.VMEM((rows, width), jnp.bfloat16),
            pltpu.VMEM((plan.slots, width), jnp.bfloat16),
            pltpu.VMEM((places, plan.slots, width), jnp.bfloat16),
            pltpu.VMEM((places, 1, plan.slots), jnp.int32),
            pltpu.VMEM((1, plan.slots), jnp.int32),
            pltpu.VMEM((G, 1, plan.slots), jnp.int32),
            pltpu.VMEM((plan.slots, 1), jnp.int32),
            pltpu.VMEM((rows, 1), jnp.int32),
            pltpu.VMEM((plan.slots, 128), jnp.float32),
            pltpu.VMEM((plan.slots, LABELS), jnp.float32),
            pltpu.VMEM((1, plan.slots), jnp.float32),
            pltpu.VMEM((G, 1, plan.slots), jnp.float32),
            pltpu.VMEM((plan.slots, LABELS), jnp.float32),
            pltpu.SemaphoreType.DMA((copies,)),
            pltpu.SemaphoreType.DMA((places, G)),
            pltpu.SemaphoreType.DMA((G,)),
            pltpu.SemaphoreType.DMA((places,)),
            pltpu.SemaphoreType.DMA((G,)),
            pltpu.SemaphoreType.DMA((G,)),
            pltpu.SemaphoreType.DMA,
        ],
        compiler_params=pltpu.CompilerParams(
            collective_id=0, has_side_effects=True, vmem_limit_bytes=48 * 1024 * 1024
        ),
    )(
        embeddings,
        centroids,
        (cluster * LABELS + labels).reshape(1, rows),
    )
    return (weight.reshape(rows), label_sums)


def solution(mesh):
    in_specs = (P(("ingest", "pair"), None), P(), P(("ingest", "pair")), P(("ingest", "pair")))
    out_specs = (P(("ingest", "pair")), P(("ingest", "pair"), None))
    return jax.shard_map(
        functools.partial(on_device, dict(mesh.shape)),
        mesh=mesh,
        in_specs=in_specs,
        out_specs=out_specs,
        check_vma=False,
    )
```

```python
import functools

import jax
import jax.numpy as jnp
from jax import lax
from jax.experimental import pallas as pl
from jax.experimental.pallas import tpu as pltpu
from jax.sharding import PartitionSpec as P

LABELS = 128
LEVELS = 32766.0
SHARPNESS = 8.0
EPSILON = 1e-06
CORES = 2
MESH = pl.DeviceIdType.MESH


class Plan:
    def __init__(self, mesh_shape, rows, width, clusters):
        self.groups = mesh_shape["ingest"]
        self.sub = mesh_shape["pair"] // self.groups
        self.xs = mesh_shape["ingest"] // CORES
        self.rows = rows
        self.width = width
        self.clusters = clusters
        self.group_clusters = clusters // self.groups
        self.cap = 2 * rows // self.groups
        self.slots = self.groups * self.cap
        self.places = self.xs * self.sub * CORES
        self.order = sorted(range(self.groups), key=lambda o: (min(o, self.groups - o), o))
        self.chunk = 256 if self.slots % 256 == 0 else 128

    def place(self, dx, dy, dc):
        return (dx % self.xs * self.sub + dy % self.sub) * CORES + dc % CORES

    def offsets(self):
        return [
            (dx, dy, dc)
            for dx in range(self.xs)
            for dy in range(self.sub)
            for dc in range(CORES)
            if dx or dy or dc
        ]


def group_of(plan, cluster):
    group = jnp.zeros(cluster.shape, jnp.int32)
    for g in range(1, plan.groups):
        group = group + (cluster >= g * plan.group_clusters).astype(jnp.int32)
    return group


def column_of(row):
    parts = []
    eye = lax.broadcasted_iota(jnp.int32, (128, 128), 0) == lax.broadcasted_iota(
        jnp.int32, (128, 128), 1
    )
    for b in range(row.shape[1] // 128):
        parts.append(
            jnp.sum(jnp.where(eye, row[:, b * 128 : (b + 1) * 128], 0), axis=1, keepdims=True)
        )
    return jnp.concatenate(parts, axis=0)


def row_of(column):
    parts = []
    eye = lax.broadcasted_iota(jnp.int32, (128, 128), 0) == lax.broadcasted_iota(
        jnp.int32, (128, 128), 1
    )
    for b in range(column.shape[0] // 128):
        parts.append(
            jnp.sum(jnp.where(eye, column[b * 128 : (b + 1) * 128, :], 0), axis=0, keepdims=True)
        )
    return jnp.concatenate(parts, axis=1)


def kernel(
    plan,
    emb_ref,
    cent_ref,
    code_ref,
    weight_ref,
    label_ref,
    emb,
    packed,
    keys,
    codes,
    code_tx,
    code_rx,
    qcol,
    poscol,
    dens_acc,
    lab_acc,
    dens_tx,
    dens_rx,
    lab_tx,
    lab_rx,
    send_sem,
    row_sem,
    code_rx_sem,
    code_sem,
    dens_sem,
    lab_sem,
    emb_sem,
):
    G, cap, slots, sub, order = plan.groups, plan.cap, plan.slots, plan.sub, plan.order
    ingest = lax.axis_index("ingest")
    pair = lax.axis_index("pair")
    x, core = ingest // CORES, ingest % CORES
    z, y = pair // sub, pair % sub

    def plane_device(dx, dy, dc):
        return (
            lax.rem(x + dx, plan.xs) * CORES + lax.rem(core + dc, CORES),
            z * sub + lax.rem(y + dy, sub),
        )

    def column_device(dz):
        return (ingest, lax.rem(z + dz, G) * sub + y)

    fetch = pltpu.make_async_copy(emb_ref, emb, emb_sem)
    fetch.start()
    barrier = pltpu.get_barrier_semaphore()
    for dz in range(1, G):
        pl.semaphore_signal(barrier, inc=1, device_id=column_device(dz), device_id_type=MESH)
    for offset in plan.offsets():
        pl.semaphore_signal(barrier, inc=1, device_id=plane_device(*offset), device_id_type=MESH)

    def slot_of(cluster, rank):
        offset = z - group_of(plan, cluster)
        offset = jnp.where(offset < 0, offset + G, offset)
        block = jnp.zeros(offset.shape, jnp.int32)
        for b in range(1, G):
            block = jnp.where(offset == order[b], b, block)
        return block * cap + rank

    rows = plan.rows
    code_row = code_ref[...]
    code_col = column_of(code_row)
    crow, ccol = code_row >> 7, code_col >> 7
    same = group_of(plan, ccol) == group_of(plan, crow)
    first = lax.broadcasted_iota(jnp.int32, (rows, rows), 0)
    second = lax.broadcasted_iota(jnp.int32, (rows, rows), 1)
    rank_row = jnp.sum(jnp.where(same & (first < second), 1, 0), axis=0, keepdims=True)
    rank_col = jnp.sum(jnp.where(same & (second < first), 1, 0), axis=1, keepdims=True)
    pos_row = slot_of(crow, rank_row)
    pos_col = slot_of(ccol, rank_col)
    poscol[...] = pos_col
    lane = lax.broadcasted_iota(jnp.int32, (rows, slots), 1)
    code_tx[...] = jnp.sum(jnp.where(pos_col == lane, code_col + 1, 0), axis=0, keepdims=True)

    lookup = (ccol == lax.broadcasted_iota(jnp.int32, (rows, plan.clusters), 1)).astype(
        jnp.float32
    ).astype(jnp.bfloat16)
    centre = jnp.dot(lookup, cent_ref[...], preferred_element_type=jnp.float32)
    fetch.wait()
    shifted = centre + emb[...].astype(jnp.float32)
    scale = lax.rsqrt(jnp.sum(shifted * shifted, axis=1, keepdims=True) + EPSILON)
    unit = (shifted * scale).astype(jnp.bfloat16)
    for b in range(G):
        pick = (
            lax.broadcasted_iota(jnp.int32, (cap, rows), 0) + b * cap == pos_row
        ).astype(jnp.float32).astype(jnp.bfloat16)
        block = jnp.dot(pick, unit, preferred_element_type=jnp.float32).astype(jnp.bfloat16)
        if b == 0:
            keys[0, pl.ds(0, cap), :] = block
        else:
            packed[pl.ds(b * cap, cap), :] = block

    pl.semaphore_wait(barrier, G - 1 + plan.places - 1)

    sent, dispatched = [], []

    def send(src, dst, sem, device):
        copy = pltpu.make_async_remote_copy(
            src_ref=src,
            dst_ref=dst,
            send_sem=send_sem.at[len(sent)],
            recv_sem=sem,
            device_id=device,
            device_id_type=MESH,
        )
        copy.start()
        sent.append(copy)

    def arrive(dst, sem):
        pltpu.make_async_remote_copy(
            src_ref=dst,
            dst_ref=dst,
            send_sem=send_sem.at[0],
            recv_sem=sem,
            device_id=column_device(1),
            device_id_type=MESH,
        ).wait_recv()

    def part(place, b, half=None):
        if half is None:
            return keys.at[place, pl.ds(b * cap, cap)]
        return keys.at[place, pl.ds(b * cap + half * (cap // 2), cap // 2)]

    def pass_on(src_place, to_place, b, device, half=None):
        send(part(src_place, b, half), part(to_place, b, half), row_sem.at[to_place, b], device)

    here = {(0, 0)}

    def rows_arrive(place, b):
        if (place, b) not in here:
            here.add((place, b))
            arrive(part(place, b), row_sem.at[place, b])

    xrange, yrange = range(1, plan.xs), range(1, sub)

    def spread(b):
        for dx in xrange:
            pass_on(0, plan.place(-dx, 0, 0), b, plane_device(dx, 0, 0))
        for dy in yrange:
            pass_on(0, plan.place(0, -dy, 0), b, plane_device(0, dy, 0))
        pass_on(0, plan.place(0, 0, 1), b, plane_device(0, 0, 1))

    def forward_near(b):
        for dx in xrange:
            rows_arrive(plan.place(dx, 0, 0), b)
            for dy in yrange:
                pass_on(
                    plan.place(dx, 0, 0), plan.place(dx, -dy, 0), b, plane_device(0, dy, 0), 0
                )
            pass_on(plan.place(dx, 0, 0), plan.place(dx, 0, 1), b, plane_device(0, 0, 1))
        for dy in yrange:
            rows_arrive(plan.place(0, dy, 0), b)
            for dx in xrange:
                pass_on(
                    plan.place(0, dy, 0), plan.place(-dx, dy, 0), b, plane_device(dx, 0, 0), 1
                )
            pass_on(plan.place(0, dy, 0), plan.place(0, dy, 1), b, plane_device(0, 0, 1))

    def forward_far(b):
        for dx in xrange:
            for dy in yrange:
                rows_arrive(plan.place(dx, dy, 0), b)
                pass_on(plan.place(dx, dy, 0), plan.place(dx, dy, 1), b, plane_device(0, 0, 1))

    def dispatch(b):
        send(
            packed.at[pl.ds(b * cap, cap)],
            part(0, b),
            row_sem.at[0, b],
            column_device(G - order[b]),
        )
        dispatched.append(sent[-1])
        return sent[-1]

    for b in range(1, G):
        send(code_tx, code_rx.at[b], code_rx_sem.at[b], column_device(G - order[b]))
    going = dispatch(1)
    spread(0)

    lane_row = lax.broadcasted_iota(jnp.int32, (1, slots), 1)

    def block_lanes(b):
        return (lane_row >= b * cap) & (lane_row < (b + 1) * cap)

    code = jnp.where(block_lanes(0), code_tx[...], 0)
    for b in range(1, G):
        arrive(code_rx.at[b], code_rx_sem.at[b])
        code = code + jnp.where(block_lanes(b), code_rx[b], 0)
    codes[0] = code
    for offset in plan.offsets():
        to = plan.place(*(-step for step in offset))
        send(codes.at[0], codes.at[to], code_sem.at[to], plane_device(*offset))
    qcol[...] = (column_of(code) - 1) >> 7
    dens_acc[...] = jnp.zeros_like(dens_acc)
    lab_acc[...] = jnp.zeros_like(lab_acc)
    for offset in plan.offsets():
        arrive(codes.at[plan.place(*offset)], code_sem.at[plan.place(*offset)])

    chunk = plan.chunk
    steps = slots // chunk

    def compute(place, first_step, last_step):
        for b in range((last_step * chunk - 1) // cap + 1):
            rows_arrive(place, b)

        def body(step, carry):
            start = pl.multiple_of(step * chunk, chunk)
            key_rows = keys[place, pl.ds(start, chunk), :]
            key_code = codes[place, :, pl.ds(start, chunk)] - 1
            scores = lax.dot_general(
                keys[0], key_rows, (((1,), (1,)), ((), ())), preferred_element_type=jnp.float32
            )
            value = jnp.where(
                qcol[...] == key_code >> 7,
                jnp.exp(SHARPNESS * scores - SHARPNESS),
                0.0,
            )
            part_sum = value[:, :128]
            for b in range(1, chunk // 128):
                part_sum = part_sum + value[:, b * 128 : (b + 1) * 128]
            dens_acc[...] += part_sum
            table = (
                lax.broadcasted_iota(jnp.int32, (LABELS, chunk), 0) == (key_code & (LABELS - 1))
            ).astype(jnp.float32).astype(jnp.bfloat16)
            lab_acc[...] += lax.dot_general(
                value.astype(jnp.bfloat16),
                table,
                (((1,), (1,)), ((), ())),
                preferred_element_type=jnp.float32,
            )
            return carry

        lax.fori_loop(first_step, last_step, body, 0, unroll=True)

    for b in range(1, G):
        going.wait_send()
        if b + 1 < G:
            going = dispatch(b + 1)
        rows_arrive(0, b)
        spread(b)
        forward_near(b - 1)
        if b >= 2:
            forward_far(b - 2)

    near = [(dx, 0) for dx in xrange] + [(0, dy) for dy in yrange]
    far = [(dx, dy) for dx in xrange for dy in yrange]
    compute(0, 0, steps)
    compute(plan.place(0, 0, 1), 0, steps)
    for dx, dy in near:
        compute(plan.place(dx, dy, 0), 0, steps - 1)
    forward_near(G - 1)
    forward_far(G - 2)
    for dx, dy in near:
        compute(plan.place(dx, dy, 1), 0, steps - 1)
    for dc in range(CORES):
        for dx, dy in far:
            compute(plan.place(dx, dy, dc), 0, steps - 1)
    for dx, dy in near:
        compute(plan.place(dx, dy, 0), steps - 1, steps)
    forward_far(G - 1)
    for dx, dy in near:
        compute(plan.place(dx, dy, 1), steps - 1, steps)
    for dc in range(CORES):
        for dx, dy in far:
            compute(plan.place(dx, dy, dc), steps - 1, steps)

    largest = jnp.maximum(jnp.max(lab_acc[...], axis=1, keepdims=True), 1e-30)
    dens_row = row_of(jnp.sum(dens_acc[...], axis=1, keepdims=True))
    largest_row = row_of(largest)
    dens_tx[:, :slots] = dens_row
    dens_tx[:, slots:] = largest_row
    lab_tx[...] = (lab_acc[...] * (LEVELS / largest) + 0.5).astype(jnp.int32).astype(jnp.int16)
    for b in range(1, G):
        send(dens_tx, dens_rx.at[b], dens_sem.at[b], column_device(order[b]))
    for b in range(1, G):
        send(
            lab_tx.at[pl.ds(b * cap, cap)],
            lab_rx.at[pl.ds(b * cap, cap)],
            lab_sem.at[b],
            column_device(order[b]),
        )
    lab_rx[pl.ds(0, cap), :] = lab_tx[pl.ds(0, cap), :]
    dens = jnp.where(block_lanes(0), dens_row, 0.0)
    unit_row = jnp.where(block_lanes(0), largest_row, 0.0)
    for b in range(1, G):
        arrive(dens_rx.at[b], dens_sem.at[b])
        dens = dens + jnp.where(block_lanes(b), dens_rx[b, :, :slots], 0.0)
        unit_row = unit_row + jnp.where(block_lanes(b), dens_rx[b, :, slots:], 0.0)
    hit = poscol[...] == lane
    weight_ref[...] = row_of(1.0 / jnp.sum(jnp.where(hit, dens, 0.0), axis=1, keepdims=True))
    unit_col = jnp.sum(jnp.where(hit, unit_row, 0.0), axis=1, keepdims=True) / LEVELS
    for b in range(1, G):
        arrive(lab_rx.at[pl.ds(b * cap, cap)], lab_sem.at[b])
    pick = hit.astype(jnp.float32).astype(jnp.bfloat16)
    rest = lab_rx[...].astype(jnp.int32).astype(jnp.float32)
    total = jnp.zeros((rows, LABELS), jnp.float32)
    for _ in range(2):
        piece = rest.astype(jnp.bfloat16)
        total = total + jnp.dot(pick, piece, preferred_element_type=jnp.float32)
        rest = rest - piece.astype(jnp.float32)
    label_ref[...] = total * unit_col
    for copy in sent:
        if not any(copy is other for other in dispatched):
            copy.wait_send()


def on_device(mesh_shape, embeddings, centroids, cluster, labels):
    rows, width = embeddings.shape
    plan = Plan(mesh_shape, rows, width, centroids.shape[0])
    G, places = plan.groups, plan.places
    near, far = plan.xs - 1 + plan.sub - 1, (plan.xs - 1) * (plan.sub - 1)
    copies = 4 * (G - 1) + places - 1 + G * (near + 1 + near + 2 * far + far)
    vmem = pl.BlockSpec(memory_space=pltpu.VMEM)
    weight, label_sums = pl.pallas_call(
        functools.partial(kernel, plan),
        out_shape=(
            jax.ShapeDtypeStruct((1, rows), jnp.float32),
            jax.ShapeDtypeStruct((rows, LABELS), jnp.float32),
        ),
        in_specs=[pl.BlockSpec(memory_space=pl.ANY), vmem, vmem],
        out_specs=(vmem, vmem),
        scratch_shapes=[
            pltpu.VMEM((rows, width), jnp.bfloat16),
            pltpu.VMEM((plan.slots, width), jnp.bfloat16),
            pltpu.VMEM((places, plan.slots, width), jnp.bfloat16),
            pltpu.VMEM((places, 1, plan.slots), jnp.int32),
            pltpu.VMEM((1, plan.slots), jnp.int32),
            pltpu.VMEM((G, 1, plan.slots), jnp.int32),
            pltpu.VMEM((plan.slots, 1), jnp.int32),
            pltpu.VMEM((rows, 1), jnp.int32),
            pltpu.VMEM((plan.slots, 128), jnp.float32),
            pltpu.VMEM((plan.slots, LABELS), jnp.float32),
            pltpu.VMEM((1, 2 * plan.slots), jnp.float32),
            pltpu.VMEM((G, 1, 2 * plan.slots), jnp.float32),
            pltpu.VMEM((plan.slots, LABELS), jnp.int16),
            pltpu.VMEM((plan.slots, LABELS), jnp.int16),
            pltpu.SemaphoreType.DMA((copies,)),
            pltpu.SemaphoreType.DMA((places, G)),
            pltpu.SemaphoreType.DMA((G,)),
            pltpu.SemaphoreType.DMA((places,)),
            pltpu.SemaphoreType.DMA((G,)),
            pltpu.SemaphoreType.DMA((G,)),
            pltpu.SemaphoreType.DMA,
        ],
        compiler_params=pltpu.CompilerParams(
            collective_id=0, has_side_effects=True, vmem_limit_bytes=48 * 1024 * 1024
        ),
    )(
        embeddings,
        centroids,
        (cluster * LABELS + labels).reshape(1, rows),
    )
    return (weight.reshape(rows), label_sums)


def solution(mesh):
    in_specs = (P(("ingest", "pair"), None), P(), P(("ingest", "pair")), P(("ingest", "pair")))
    out_specs = (P(("ingest", "pair")), P(("ingest", "pair"), None))
    return jax.shard_map(
        functools.partial(on_device, dict(mesh.shape)),
        mesh=mesh,
        in_specs=in_specs,
        out_specs=out_specs,
        check_vma=False,
    )
```
